32 devices in a mesh: groups: 2 (over x), tm: 16 (over z, y, core).
Axes of the slice: x: 2, y: 2, z: 4, core: 2. Of those that a mesh axis runs over, the one named last changes fastest.
Arguments:
- raw: bfloat16 [32768, 3072], P('tm', 'groups'), parts along dimension 1, may hold values from -6 to 6
- taps: float32 [61], replicated, may hold values from -1.5 to 1.5
- whiten: float32 [3072, 33], P('groups'), parts along dimension 0, may hold values from -1.2 to 1.2
- templates: bfloat16 [512, 2048], P('groups'), parts along dimension 0, may hold values from -0.29882812 to 0.29882812
- template_base: int32 [512], P('groups'), parts along dimension 0, may hold values from 0 to 1472, as said below
- amp_scale: float32 [16], P('groups'), parts along dimension 0, may hold values from 0.5 to 2
- spike_time: int32 [32768], P(('groups', 'tm')), parts along dimension 0, may hold values from 0 to 2047, as said below
- spike_template: int32 [32768], P(('groups', 'tm')), parts along dimension 0, may hold values from 0 to 255, as said below
- spike_session: int32 [32768], P(('groups', 'tm')), parts along dimension 0, may hold values from 0 to 7
- live_count: int32 [32], P(('groups', 'tm')), parts along dimension 0, may hold values from 128 to 1024, as said below
Outputs:
- whitened: bfloat16 [32768, 3072], P('tm', 'groups'), parts along dimension 1
- amplitudes: float32 [32768], P(('groups', 'tm')), parts along dimension 0
- new_templates: float32 [512, 2048], P(('groups', 'tm')), parts along dimension 0
The draws below stay inside these ranges and needn't reach their ends.
There are 2 independent parts, one for each index of `groups`. The reference program is written for one: setup_inputs(seed, part) draws one part's arguments, and reference() takes and returns one part's arrays. A program takes and returns all parts, laid end to end along the dimension named above; an argument that names none is the same for every part. Nothing has to cross between parts.
Inputs may be any that keep to these rules, and one draw needn't show every extreme that they name: `template_base`: each template's 64 channels lie within one probe; some template starts at channel 1536 - 64. `live_count`: some time block has all 1024 slots live. `spike_template`: the spike slots of one time block name at most 8 distinct templates among templates j * 16 to j * 16 + 15, for every j; some block names exactly 8 of them for some j. `spike_time`: in every time block one live slot lies at sample 0 and another at sample 2048 - 1.
All inputs are finite; a program needn't handle non-finite values.
Results may differ from the reference program's by a relative error of at most 0.011.
Values may be sent and summed in bfloat16 or wider, within the bound.
A program may use at most 192 MiB of HBM per device.

```python
import math
import jax
import jax.numpy as jnp
from jax import lax

CH_PROBE = 384
PROBES = 4
TAPS = 61
BAND = 33
TW = 32
NB = 64
TEMP_DEV = 16
NSESS = 8
T_DEV = 2048
SPK_DEV = 1024
CAP = 8
CH = 1536
NBLK = 16
TIME = 32768
SPIKES = 16384
NTEMP = 256


def draw_template_base(key, part):
    key_probe = jax.random.fold_in(key, 11)
    key_off = jax.random.fold_in(key, 12)
    key_pos = jax.random.fold_in(key, 13)
    probe = jax.random.randint(key_probe, (NTEMP,), 0, PROBES)
    offset = jax.random.randint(key_off, (NTEMP,), 0, CH_PROBE - NB + 1)
    base = probe * CH_PROBE + offset
    where_top = jax.random.randint(key_pos, (), 0, NTEMP)
    base = jnp.where(jnp.arange(NTEMP) == where_top, CH - NB, base)
    return base.astype(jnp.int32)


def draw_live_count(key, part):
    key_counts = jax.random.fold_in(key, 21)
    key_pos = jax.random.fold_in(key, 22)
    counts = jax.random.randint(key_counts, (NBLK,), SPK_DEV // 8, SPK_DEV + 1)
    where_full = jax.random.randint(key_pos, (), 0, NBLK)
    counts = jnp.where(jnp.arange(NBLK) == where_full, SPK_DEV, counts)
    return counts.astype(jnp.int32)


def draw_spike_time(key, part):
    key_times = jax.random.fold_in(key, 41)
    key_low = jax.random.fold_in(key, 42)
    key_gap = jax.random.fold_in(key, 43)
    sure = SPK_DEV // 8
    times = jax.random.randint(key_times, (NBLK, SPK_DEV), 0, T_DEV)
    low_slot = jax.random.randint(key_low, (NBLK, 1), 0, sure)
    gap = jax.random.randint(key_gap, (NBLK, 1), 0, sure - 1)
    high_slot = (low_slot + 1 + gap) % sure
    within = jnp.arange(SPK_DEV)[None, :]
    times = jnp.where(within == low_slot, 0, times)
    times = jnp.where(within == high_slot, T_DEV - 1, times)
    return times.reshape(SPIKES).astype(jnp.int32)


def draw_spike_template(key, part):
    key_first = jax.random.fold_in(key, 31)
    key_second = jax.random.fold_in(key, 32)
    key_order = jax.random.fold_in(key, 33)
    key_pick = jax.random.fold_in(key, 34)
    key_which = jax.random.fold_in(key, 35)
    slots = jnp.arange(SPIKES)
    block = slots // SPK_DEV
    within = slots % SPK_DEV
    first = jax.random.randint(key_first, (SPIKES,), 0, NBLK)
    second = jax.random.randint(key_second, (SPIKES,), 0, NBLK)
    ranked = first * second // NBLK
    order = jax.random.permutation(key_order, NBLK)
    owner = order[ranked]
    owner = jnp.where(within < CAP, block % NBLK, owner)
    pick_keys = jax.random.split(key_pick, NBLK * NBLK)
    perms = jax.vmap(lambda one_key: jax.random.permutation(one_key, TEMP_DEV))(pick_keys)
    perms = perms.reshape(NBLK, NBLK, TEMP_DEV)
    which = jax.random.randint(key_which, (SPIKES,), 0, CAP)
    which = jnp.where(within < CAP, within, which)
    local = perms[block, owner, which]
    return (owner * TEMP_DEV + local).astype(jnp.int32)


def plant(values, stream_key, least, high):
    longest = values.shape.index(max(values.shape))
    spots = []
    for shift in (0, 1):
        where = [jax.random.randint(jax.random.fold_in(stream_key, axis), (), 0, length) for axis, length in enumerate(values.shape)]
        where[longest] = (where[longest] + shift) % values.shape[longest]
        spots.append(tuple(where))
    return values.at[spots[0]].set(least).at[spots[1]].set(high)


def steps_of(own_key, shape, cuts, low, largest):
    gain, own = 1.0, jax.random.fold_in(own_key, 6)
    for dim, blocks in cuts:
        draws = jnp.exp(jax.random.uniform(jax.random.fold_in(own, dim), (blocks,), jnp.float32, low / len(cuts), largest / len(cuts)))
        gain = gain * jnp.repeat(draws, shape[dim] // blocks).reshape([-1 if axis == dim else 1 for axis in range(len(shape))])
    return gain


def centred(stream_key, dims, spread, reach, cuts=(), kind=jnp.bfloat16):
    loudness = steps_of(stream_key, dims, cuts, -0.22, 0.18) if cuts else 1.0
    drawn = jax.random.normal(stream_key, dims, jnp.float32) * spread * loudness
    return jnp.minimum(jnp.maximum(drawn, -reach), reach).astype(kind)


def setup_inputs(seed: int = 0, part: int = 0) -> dict:
    splits = jax.random.split(jax.random.key(seed), 11)
    part_keys = jax.random.split(jax.random.fold_in(splits[10], part), 11)
    raw = centred(part_keys[0], (TIME, CH), 1.0, 6.0, ((0, 16),))
    taps = centred(splits[1], (TAPS,), 0.25, 1.5, (), jnp.float32)
    whiten = centred(part_keys[2], (CH, BAND), 0.2, 1.2, (), jnp.float32)
    templates = centred(part_keys[3], (NTEMP, TW * NB), 0.05, 0.29882812)
    template_base = draw_template_base(jax.random.fold_in(jax.random.fold_in(splits[10], part), 71), part)
    amp_scale = jnp.clip(jnp.exp(jax.random.uniform(part_keys[5], (NSESS,), jnp.float32, math.log(0.5), math.log(2.0))), 0.5, 2.0)
    spike_time = draw_spike_time(jax.random.fold_in(jax.random.fold_in(splits[10], part), 71), part)
    spike_template = draw_spike_template(jax.random.fold_in(jax.random.fold_in(splits[10], part), 71), part)
    spike_session = plant(jax.random.randint(part_keys[8], (SPIKES,), 0, NSESS), jax.random.fold_in(part_keys[8], 1), 0, NSESS - 1).astype(jnp.int32)
    live_count = draw_live_count(jax.random.fold_in(jax.random.fold_in(splits[10], part), 71), part)
    return dict(raw=raw, taps=taps, whiten=whiten, templates=templates, template_base=template_base, amp_scale=amp_scale, spike_time=spike_time, spike_template=spike_template, spike_session=spike_session, live_count=live_count)


def build_mixer(whiten):
    half_band = BAND // 2
    rows_in = jnp.arange(CH_PROBE)[:, None, None]
    rows_out = jnp.arange(CH_PROBE)[None, :, None]
    offsets = jnp.arange(BAND)[None, None, :]
    selector = (rows_in - rows_out + half_band == offsets).astype(jnp.float32)
    per_probe = whiten.reshape(PROBES, CH_PROBE, BAND)
    mixer = jnp.einsum('poj,ioj->pio', per_probe, selector, precision=lax.Precision.HIGHEST)
    return mixer.astype(jnp.bfloat16)


def reference(raw, taps, whiten, templates, template_base, amp_scale, spike_time, spike_template, spike_session, live_count):
    half_taps = TAPS // 2
    taps_b = taps.astype(jnp.bfloat16).astype(jnp.float32)
    padded = jnp.pad(raw, ((half_taps, half_taps), (0, 0)))
    filtered = jnp.zeros((TIME, CH), jnp.float32)
    for k in range(TAPS):
        filtered = filtered + taps_b[k] * padded[k:k + TIME].astype(jnp.float32)
    filtered = filtered.astype(jnp.bfloat16)
    mixer = build_mixer(whiten)
    white = jnp.einsum('npi,pio->npo', filtered.reshape(TIME, PROBES, CH_PROBE).astype(jnp.float32), mixer.astype(jnp.float32))
    white = white.reshape(TIME, CH).astype(jnp.bfloat16)
    rim = TW // 2
    wpad = jnp.pad(white, ((rim, rim), (0, 0)))
    slots = jnp.arange(SPIKES, dtype=jnp.int32)
    block = slots // SPK_DEV
    start = (block * T_DEV + spike_time).astype(jnp.int32)
    base = template_base[spike_template].astype(jnp.int32)

    def extract(row, col):
        return lax.dynamic_slice(wpad, (row, col), (TW, NB)).reshape(TW * NB)

    snippet = jax.vmap(extract)(start, base).astype(jnp.float32)
    tmpl = templates.astype(jnp.float32)
    energy_t = jnp.sum(tmpl * tmpl, axis=1)
    chosen = tmpl[spike_template]
    inner = jnp.sum(snippet * chosen, axis=1)
    scale = amp_scale[spike_session]
    live = (slots % SPK_DEV) < live_count[block]
    amplitudes = jnp.where(live, scale * inner / (energy_t[spike_template] + 1e-5), 0.0)
    term = (amplitudes[:, None] * (snippet - amplitudes[:, None] * chosen)).astype(jnp.bfloat16)
    grads = jax.ops.segment_sum(term.astype(jnp.float32), spike_template, num_segments=NTEMP)
    weight = jax.ops.segment_sum(amplitudes * amplitudes, spike_template, num_segments=NTEMP)
    new_templates = tmpl + grads / (weight[:, None] + 1.0)
    return white, amplitudes, new_templates
```

```python
import jax
import jax.numpy as jnp
from jax import lax
from jax.experimental import pallas as pl
from jax.experimental.pallas import tpu as pltpu
from jax.sharding import PartitionSpec as P

CH_PROBE = 384
BAND = 33
TW = 32
NB = 64
TEMP_DEV = 16
CAP = 8
TILE = 256
HALO = 48
GROUP = 16
PACK = CAP * TW // 2 + 2 * CAP


def from_neighbours(low_part, high_part, axis):
    count = lax.axis_size(axis)
    forward = [(i, i + 1) for i in range(count - 1)]
    backward = [(target, source) for source, target in forward]
    return lax.ppermute(low_part, axis, forward), lax.ppermute(high_part, axis, backward)


def body(
    time_s,
    tmpl_s,
    slot_s,
    quot_s,
    rest_s,
    used_s,
    edge_s,
    raw_ref,
    prev_ref,
    next_ref,
    low_ref,
    high_ref,
    taps_ref,
    whiten_ref,
    temp_ref,
    coef_ref,
    white_ref,
    amp_ref,
    pack_ref,
    wide,
    toep,
    mixer,
    placed,
    sums,
    squares,
):
    i = pl.program_id(0)
    last = pl.num_programs(0) - 1
    width = raw_ref.shape[1]
    lanes = width // 128
    probes = width // CH_PROBE
    slots = placed.shape[0]
    rows = wide.shape[1] - TW

    lane = lax.broadcasted_iota(jnp.int32, (TW, 128), 1)

    @pl.when(i == 0)
    def _():
        spread = jnp.broadcast_to(taps_ref[...], (TILE, taps_ref.shape[1]))
        skewed = pltpu.roll(spread, 0, 1, stride=1, stride_axis=0)
        toep[...] = skewed.astype(jnp.bfloat16)
        for p in range(probes):
            part = whiten_ref[p * CH_PROBE : (p + 1) * CH_PROBE, :]
            part = jnp.concatenate([part, jnp.zeros((CH_PROBE, 384), jnp.float32)], axis=1)
            skewed = pltpu.roll(part, 512 - BAND // 2, 1, stride=1, stride_axis=0)
            mixer[p] = skewed[:, :CH_PROBE].T.astype(jnp.bfloat16)

    def whitened(segment, band):
        filtered = jnp.dot(band, segment, preferred_element_type=jnp.float32).astype(jnp.bfloat16)
        return [
            jnp.dot(
                filtered[:, p * CH_PROBE : (p + 1) * CH_PROBE],
                mixer[p],
                preferred_element_type=jnp.float32,
            ).astype(jnp.bfloat16)
            for p in range(probes)
        ]

    def keep(parts, start, size, scale=None):
        whole = jnp.concatenate(parts, axis=1).astype(jnp.float32)
        if scale is not None:
            whole = whole * scale
        for c in range(lanes):
            wide[c, pl.ds(start, size), :] = whole[:, c * 128 : (c + 1) * 128]

    prev = jnp.where(i == 0, low_ref[HALO - 32 :, :], prev_ref[...])
    after = jnp.where(i == last, high_ref[:32, :], next_ref[...])
    segment = jnp.concatenate([prev, raw_ref[...], after], axis=0)
    parts = whitened(segment, toep[:, : TILE + 64])
    for p in range(probes):
        white_ref[:, p * CH_PROBE : (p + 1) * CH_PROBE] = parts[p]
    keep(parts, pl.multiple_of(16 + i * TILE, 16), TILE)

    @pl.when(i == 0)
    def _():
        segment = jnp.concatenate([low_ref[...], raw_ref[:32, :]], axis=0)
        inside = edge_s[0].astype(jnp.float32)
        keep(whitened(segment, toep[:16, : HALO + 32]), 0, 16, inside)

    @pl.when(i == last)
    def _():
        segment = jnp.concatenate([raw_ref[TILE - 32 :, :], high_ref[...]], axis=0)
        inside = edge_s[1].astype(jnp.float32)
        keep(whitened(segment, toep[:16, : HALO + 32]), rows + 16, 16, inside)

        @pl.loop(0, slots // 4)
        def _(four):
            for j in range(4):
                slot = four * 4 + j
                k = used_s[slot]
                r = rest_s[k]
                rolled = pltpu.roll(temp_ref[k].astype(jnp.float32), lax.rem(r, 128), 1)
                for half in range(2):
                    at = lane + 128 * half - r
                    placed[slot, half] = jnp.where((at >= 0) & (at < NB), rolled, 0.0)
                    sums[slot, half] = jnp.zeros((TW, 128), jnp.float32)

        squares[...] = jnp.zeros_like(squares)

        @pl.loop(0, amp_ref.shape[0] // GROUP)
        def _(group):
            first = pl.multiple_of(group * GROUP, GROUP)
            windows, places, folded = [], [], []
            for j in range(GROUP):
                k = tmpl_s[first + j]
                slot = slot_s[k]
                window = wide[pl.ds(quot_s[k], 2), pl.ds(time_s[first + j], TW), :]
                product = window * placed[slot]
                total = product[0] + product[1]
                folded.append(jnp.sum(total, axis=0, keepdims=True))
                windows.append(window)
                places.append(slot)
            inner = jnp.sum(jnp.concatenate(folded, axis=0), axis=1, keepdims=True)
            amps = coef_ref[pl.ds(first, GROUP), :] * inner
            amp_ref[pl.ds(first, GROUP), :] = amps
            for j in range(GROUP):
                one = amps[j : j + 1, :]
                sums[places[j]] += one[None] * windows[j]
                squares[pl.ds(places[j], 1), :] += jnp.broadcast_to(one * one, (1, 128))

        half_lane = lane[: TW // 2]
        aux_lane = lane[:CAP]
        aux_row = lax.broadcasted_iota(jnp.int32, (CAP, 128), 0)

        @pl.loop(0, slots // CAP)
        def _(owner):
            start = pl.multiple_of(owner * PACK, 16)
            names = jnp.zeros((CAP, 128), jnp.float32)
            for j in range(CAP):
                slot = owner * CAP + j
                k = used_s[slot]
                r = rest_s[k]
                merged = jnp.where(lane >= r, sums[slot, 0], sums[slot, 1])
                merged = jnp.where(r >= 128, sums[slot, 1], merged)
                back = pltpu.roll(merged, lax.rem(256 - r, 128), 1)
                lower = back[TW // 2 :]
                both = jnp.where(half_lane < NB, back[: TW // 2], pltpu.roll(lower, NB, 1))
                pack_ref[pl.ds(pl.multiple_of(start + j * 16, 16), 16), :] = both.astype(
                    jnp.bfloat16
                )
                name = (k - owner * TEMP_DEV).astype(jnp.float32)
                names = jnp.where(aux_row == j, name, names)
            aux = squares[pl.ds(pl.multiple_of(owner * CAP, CAP), CAP), :]
            aux = jnp.where(aux_lane == 1, names, aux)
            high = aux.astype(jnp.bfloat16)
            rest = (aux - high.astype(jnp.float32)).astype(jnp.bfloat16)
            both = jnp.concatenate([high.astype(jnp.float32), rest.astype(jnp.float32)], axis=0)
            pack_ref[pl.ds(pl.multiple_of(start + CAP * 16, 16), 16), :] = both.astype(jnp.bfloat16)


def shards(
    raw,
    taps,
    whiten,
    templates,
    template_base,
    amp_scale,
    spike_time,
    spike_template,
    spike_session,
    live_count,
):
    rows, width = raw.shape
    spikes = spike_time.shape[0]
    ntemp = templates.shape[0]
    position = lax.axis_index("tm")
    owners = lax.axis_size("tm")
    slots = owners * CAP
    low, high = from_neighbours(raw[rows - HALO :], raw[:HALO], "tm")
    edges = jnp.stack([position > 0, position < owners - 1]).astype(jnp.int32)

    taps_b = taps.astype(jnp.bfloat16).astype(jnp.float32)
    taps_row = jnp.pad(taps_b, (2, 384 - 2 - taps.shape[0]))[None, :]
    whiten_wide = jnp.pad(whiten, ((0, 0), (0, 128 - BAND)))
    temp_wide = jnp.pad(templates.reshape(ntemp, TW, NB), ((0, 0), (0, 0), (0, 128 - NB)))
    quot = jnp.minimum(template_base // 128, width // 128 - 2)
    rest = template_base - quot * 128

    tmpl = templates.astype(jnp.float32)
    energy_t = jnp.sum(tmpl * tmpl, axis=1)
    named = spike_template[:, None] == jnp.arange(ntemp)[None, :]
    energy = jnp.sum(jnp.where(named, energy_t[None, :], 0.0), axis=1)
    present = jnp.any(named, axis=0).reshape(owners, TEMP_DEV)
    local = jnp.arange(TEMP_DEV)
    before = local[:, None] < local[None, :]
    rank = jnp.sum(jnp.where(before[None], present[:, :, None].astype(jnp.int32), 0), axis=1)
    owner_ids = jnp.arange(owners)
    slot_of = jnp.where(present, owner_ids[:, None] * CAP + rank, 0).reshape(ntemp)
    hits = present[:, None, :] & (rank[:, None, :] == jnp.arange(CAP)[None, :, None])
    used = jnp.sum(jnp.where(hits, local[None, None, :], 0), axis=2)
    used = (used + owner_ids[:, None] * TEMP_DEV).reshape(slots)

    sessions = jnp.arange(amp_scale.shape[0])
    scale = jnp.sum(
        jnp.where(spike_session[:, None] == sessions[None, :], amp_scale[None, :], 0.0), axis=1
    )
    live = jnp.arange(spikes) < live_count[0]
    coef = jnp.where(live, scale / (energy + 1e-05), 0.0)[:, None]

    step = TILE // 32
    final = rows // 32 - 1
    fixed2 = lambda i, *_: (0, 0)
    white, amps, packed = pl.pallas_call(
        body,
        grid_spec=pltpu.PrefetchScalarGridSpec(
            num_scalar_prefetch=7,
            grid=(rows // TILE,),
            in_specs=[
                pl.BlockSpec((TILE, width), lambda i, *_: (i, 0)),
                pl.BlockSpec((32, width), lambda i, *_: (jnp.maximum(i * step - 1, 0), 0)),
                pl.BlockSpec((32, width), lambda i, *_: (jnp.minimum((i + 1) * step, final), 0)),
                pl.BlockSpec((HALO, width), fixed2),
                pl.BlockSpec((HALO, width), fixed2),
                pl.BlockSpec((1, 384), fixed2),
                pl.BlockSpec((width, 128), fixed2),
                pl.BlockSpec((ntemp, TW, 128), lambda i, *_: (0, 0, 0)),
                pl.BlockSpec((spikes, 1), fixed2),
            ],
            out_specs=[
                pl.BlockSpec((TILE, width), lambda i, *_: (i, 0)),
                pl.BlockSpec((spikes, 1), fixed2),
                pl.BlockSpec((owners * PACK, 128), fixed2),
            ],
            scratch_shapes=[
                pltpu.VMEM((width // 128, rows + TW, 128), jnp.float32),
                pltpu.VMEM((TILE, 384), jnp.bfloat16),
                pltpu.VMEM((width // CH_PROBE, CH_PROBE, CH_PROBE), jnp.bfloat16),
                pltpu.VMEM((slots, 2, TW, 128), jnp.float32),
                pltpu.VMEM((slots, 2, TW, 128), jnp.float32),
                pltpu.VMEM((slots, 128), jnp.float32),
            ],
        ),
        out_shape=[
            jax.ShapeDtypeStruct((rows, width), jnp.bfloat16),
            jax.ShapeDtypeStruct((spikes, 1), jnp.float32),
            jax.ShapeDtypeStruct((owners * PACK, 128), jnp.bfloat16),
        ],
        compiler_params=pltpu.CompilerParams(
            dimension_semantics=("arbitrary",), vmem_limit_bytes=56 * 1024 * 1024
        ),
    )(
        spike_time,
        spike_template,
        slot_of,
        quot,
        rest,
        used,
        edges,
        raw,
        raw,
        raw,
        low,
        high,
        taps_row,
        whiten_wide,
        temp_wide,
        coef,
    )

    arrived = lax.all_to_all(packed.reshape(owners, PACK, 128), "tm", 0, 0)
    body_rows = CAP * TW // 2
    grads = arrived[:, :body_rows].reshape(owners * CAP, TW // 2 * 128)
    aux = arrived[:, body_rows:, :2].astype(jnp.float32).reshape(owners, 2, CAP, 2)
    weight = (aux[:, 0, :, 0] + aux[:, 1, :, 0]).reshape(slots)
    names = aux[:, 0, :, 1].reshape(slots).astype(jnp.int32)
    pick = local[:, None] == names[None, :]
    total = jnp.dot(pick.astype(jnp.bfloat16), grads, preferred_element_type=jnp.float32)
    total = total.reshape(TEMP_DEV, TW // 2, 2, NB).transpose(0, 2, 1, 3)
    total = total.reshape(TEMP_DEV, TW * NB)
    weights = jnp.sum(jnp.where(pick, weight[None, :], 0.0), axis=1)
    mine = lax.dynamic_slice_in_dim(templates, position * TEMP_DEV, TEMP_DEV, 0)
    new_templates = (mine.astype(jnp.float32) + total) / (weights[:, None] + 1.0)
    return white, amps.reshape(spikes), new_templates


def solution(mesh):
    placed = (
        P("tm", "groups"),
        P(),
        P("groups", None),
        P("groups", None),
        P("groups"),
        P("groups"),
        P(("groups", "tm")),
        P(("groups", "tm")),
        P(("groups", "tm")),
        P(("groups", "tm")),
    )
    return jax.shard_map(
        shards,
        mesh=mesh,
        in_specs=placed,
        out_specs=(P("tm", "groups"), P(("groups", "tm")), P(("groups", "tm"), None)),
        check_vma=False,
    )
```

```python
import jax
import jax.numpy as jnp
from jax import lax
from jax.experimental import pallas as pl
from jax.experimental.pallas import tpu as pltpu
from jax.sharding import PartitionSpec as P

CH_PROBE = 384
BAND = 33
TW = 32
NB = 64
TEMP_DEV = 16
CAP = 8
TILE = 256
HALO = 48
GROUP = 64
PACK = CAP * TW // 2 + 2 * CAP


def from_neighbours(low_part, high_part, axis):
    count = lax.axis_size(axis)
    forward = [(i, i + 1) for i in range(count - 1)]
    backward = [(target, source) for source, target in forward]
    return lax.ppermute(low_part, axis, forward), lax.ppermute(high_part, axis, backward)


def body(
    time_s,
    tmpl_s,
    slot_s,
    quot_s,
    rest_s,
    used_s,
    edge_s,
    raw_ref,
    prev_ref,
    next_ref,
    low_ref,
    high_ref,
    taps_ref,
    whiten_ref,
    temp_ref,
    coef_ref,
    white_ref,
    amp_ref,
    pack_ref,
    wide,
    toep,
    mixer,
    placed,
    sums,
    squares,
    band_rows,
    woven,
    amp_cols,
):
    i = pl.program_id(0)
    last = pl.num_programs(0) - 1
    width = raw_ref.shape[1]
    tiles = width // NB - 1
    probes = width // CH_PROBE
    slots = placed.shape[0]
    rows = wide.shape[1] - TW

    lane = lax.broadcasted_iota(jnp.int32, (TW, 128), 1)

    @pl.when(i == 0)
    def _():
        spread = jnp.broadcast_to(taps_ref[...], (TILE, taps_ref.shape[1]))
        skewed = pltpu.roll(spread, 0, 1, stride=1, stride_axis=0)
        toep[...] = skewed.astype(jnp.bfloat16)
        band_rows[...] = jnp.zeros_like(band_rows)
        band_rows[:BAND, :] = whiten_ref[...]
        for p in range(probes):
            part = band_rows[:, p * CH_PROBE : (p + 1) * CH_PROBE].T
            part = jnp.concatenate([part, jnp.zeros((CH_PROBE, 384), jnp.float32)], axis=1)
            skewed = pltpu.roll(part, 512 - BAND // 2, 1, stride=1, stride_axis=0)
            mixer[p] = skewed[:, :CH_PROBE].T.astype(jnp.bfloat16)

    def whitened(segment, band):
        filtered = jnp.dot(band, segment, preferred_element_type=jnp.float32).astype(jnp.bfloat16)
        return [
            jnp.dot(
                filtered[:, p * CH_PROBE : (p + 1) * CH_PROBE],
                mixer[p],
                preferred_element_type=jnp.float32,
            ).astype(jnp.bfloat16)
            for p in range(probes)
        ]

    def keep(parts, start, size, scale=None):
        whole = jnp.concatenate(parts, axis=1).astype(jnp.float32)
        if scale is not None:
            whole = whole * scale
        for c in range(tiles):
            wide[c, pl.ds(start, size), :] = whole[:, c * NB : c * NB + 128]

    prev = jnp.where(i == 0, low_ref[HALO - 32 :, :], prev_ref[...])
    after = jnp.where(i == last, high_ref[:32, :], next_ref[...])
    segment = jnp.concatenate([prev, raw_ref[...], after], axis=0)
    parts = whitened(segment, toep[:, : TILE + 64])
    for p in range(probes):
        white_ref[:, p * CH_PROBE : (p + 1) * CH_PROBE] = parts[p]
    keep(parts, pl.multiple_of(16 + i * TILE, 16), TILE)

    @pl.when(i == 0)
    def _():
        segment = jnp.concatenate([low_ref[...], raw_ref[:32, :]], axis=0)
        inside = edge_s[0].astype(jnp.float32)
        keep(whitened(segment, toep[:16, : HALO + 32]), 0, 16, inside)

    @pl.when(i == last)
    def _():
        segment = jnp.concatenate([raw_ref[TILE - 32 :, :], high_ref[...]], axis=0)
        inside = edge_s[1].astype(jnp.float32)
        keep(whitened(segment, toep[:16, : HALO + 32]), rows + 16, 16, inside)

        @pl.loop(0, slots // 4)
        def _(four):
            for j in range(4):
                slot = four * 4 + j
                k = used_s[slot]
                r = rest_s[k]
                pairs = temp_ref[k].astype(jnp.float32)
                woven[j, pl.ds(0, TW // 2, stride=2), :] = pairs
                woven[j, pl.ds(1, TW // 2, stride=2), :] = pltpu.roll(pairs, NB, 1)
                rolled = pltpu.roll(woven[j], r, 1)
                at = lane - r
                placed[slot] = jnp.where((at >= 0) & (at < NB), rolled, 0.0)
                sums[slot] = jnp.zeros((TW, 128), jnp.float32)

        squares[...] = jnp.zeros_like(squares)

        @pl.loop(0, amp_cols.shape[0] // GROUP)
        def _(group):
            first = pl.multiple_of(group * GROUP, GROUP)
            windows, places, folded = [], [], []
            for j in range(GROUP):
                k = tmpl_s[first + j]
                slot = slot_s[k]
                window = wide[quot_s[k], pl.ds(time_s[first + j], TW), :]
                folded.append(jnp.sum(window * placed[slot], axis=0, keepdims=True))
                windows.append(window)
                places.append(slot)
            inner = jnp.sum(jnp.concatenate(folded, axis=0), axis=1, keepdims=True)
            amps = coef_ref[pl.ds(first, GROUP), :] * inner
            amp_cols[pl.ds(first, GROUP), :] = jnp.broadcast_to(amps, (GROUP, 128))
            for j in range(GROUP):
                one = amps[j : j + 1, :]
                sums[places[j]] += one * windows[j]
                squares[pl.ds(places[j], 1), :] += jnp.broadcast_to(one * one, (1, 128))

        for b in range(amp_ref.shape[0]):
            amp_ref[b : b + 1, :] = amp_cols[b * 128 : (b + 1) * 128, :].T[:1, :]

        half_lane = lane[: TW // 2]
        aux_lane = lane[:CAP]
        aux_row = lax.broadcasted_iota(jnp.int32, (CAP, 128), 0)

        @pl.loop(0, slots // CAP)
        def _(owner):
            start = pl.multiple_of(owner * PACK, 16)
            names = jnp.zeros((CAP, 128), jnp.float32)
            for j in range(CAP):
                slot = owner * CAP + j
                k = used_s[slot]
                r = rest_s[k]
                back = pltpu.roll(sums[slot], lax.rem(128 - r, 128), 1)
                lower = back[TW // 2 :]
                both = jnp.where(half_lane < NB, back[: TW // 2], pltpu.roll(lower, NB, 1))
                pack_ref[pl.ds(pl.multiple_of(start + j * 16, 16), 16), :] = both.astype(
                    jnp.bfloat16
                )
                name = (k - owner * TEMP_DEV).astype(jnp.float32)
                names = jnp.where(aux_row == j, name, names)
            aux = squares[pl.ds(pl.multiple_of(owner * CAP, CAP), CAP), :]
            aux = jnp.where(aux_lane == 1, names, aux)
            high = aux.astype(jnp.bfloat16)
            rest = (aux - high.astype(jnp.float32)).astype(jnp.bfloat16)
            both = jnp.concatenate([high.astype(jnp.float32), rest.astype(jnp.float32)], axis=0)
            pack_ref[pl.ds(pl.multiple_of(start + CAP * 16, 16), 16), :] = both.astype(jnp.bfloat16)


def shards(
    raw,
    taps,
    whiten,
    templates,
    template_base,
    amp_scale,
    spike_time,
    spike_template,
    spike_session,
    live_count,
):
    rows, width = raw.shape
    spikes = spike_time.shape[0]
    ntemp = templates.shape[0]
    position = lax.axis_index("tm")
    owners = lax.axis_size("tm")
    slots = owners * CAP
    low, high = from_neighbours(raw[rows - HALO :], raw[:HALO], "tm")
    edges = jnp.stack([position > 0, position < owners - 1]).astype(jnp.int32)

    taps_b = taps.astype(jnp.bfloat16).astype(jnp.float32)
    taps_row = jnp.pad(taps_b, (2, 384 - 2 - taps.shape[0]))[None, :]
    temp_pairs = templates.reshape(ntemp, TW // 2, 2 * NB)
    quot = jnp.minimum(template_base // NB, width // NB - 2)
    rest = template_base - quot * NB

    tmpl = templates.astype(jnp.float32)
    energy_t = jnp.sum(tmpl * tmpl, axis=1)
    named = spike_template[:, None] == jnp.arange(ntemp)[None, :]
    energy = jnp.sum(jnp.where(named, energy_t[None, :], 0.0), axis=1)
    present = jnp.any(named, axis=0).reshape(owners, TEMP_DEV)
    local = jnp.arange(TEMP_DEV)
    before = local[:, None] < local[None, :]
    rank = jnp.sum(jnp.where(before[None], present[:, :, None].astype(jnp.int32), 0), axis=1)
    owner_ids = jnp.arange(owners)
    slot_of = jnp.where(present, owner_ids[:, None] * CAP + rank, 0).reshape(ntemp)
    hits = present[:, None, :] & (rank[:, None, :] == jnp.arange(CAP)[None, :, None])
    used = jnp.sum(jnp.where(hits, local[None, None, :], 0), axis=2)
    used = (used + owner_ids[:, None] * TEMP_DEV).reshape(slots)

    sessions = jnp.arange(amp_scale.shape[0])
    scale = jnp.sum(
        jnp.where(spike_session[:, None] == sessions[None, :], amp_scale[None, :], 0.0), axis=1
    )
    live = jnp.arange(spikes) < live_count[0]
    coef = jnp.where(live, scale / (energy + 1e-05), 0.0)[:, None]

    step = TILE // 32
    final = rows // 32 - 1
    fixed2 = lambda i, *_: (0, 0)
    white, amps, packed = pl.pallas_call(
        body,
        grid_spec=pltpu.PrefetchScalarGridSpec(
            num_scalar_prefetch=7,
            grid=(rows // TILE,),
            in_specs=[
                pl.BlockSpec((TILE, width), lambda i, *_: (i, 0)),
                pl.BlockSpec((32, width), lambda i, *_: (jnp.maximum(i * step - 1, 0), 0)),
                pl.BlockSpec((32, width), lambda i, *_: (jnp.minimum((i + 1) * step, final), 0)),
                pl.BlockSpec((HALO, width), fixed2),
                pl.BlockSpec((HALO, width), fixed2),
                pl.BlockSpec((1, 384), fixed2),
                pl.BlockSpec((BAND, width), fixed2),
                pl.BlockSpec((ntemp, TW // 2, 128), lambda i, *_: (0, 0, 0)),
                pl.BlockSpec((spikes, 1), fixed2),
            ],
            out_specs=[
                pl.BlockSpec((TILE, width), lambda i, *_: (i, 0)),
                pl.BlockSpec((spikes // 128, 128), fixed2),
                pl.BlockSpec((owners * PACK, 128), fixed2),
            ],
            scratch_shapes=[
                pltpu.VMEM((width // NB - 1, rows + TW, 128), jnp.float32),
                pltpu.VMEM((TILE, 384), jnp.bfloat16),
                pltpu.VMEM((width // CH_PROBE, CH_PROBE, CH_PROBE), jnp.bfloat16),
                pltpu.VMEM((slots, TW, 128), jnp.float32),
                pltpu.VMEM((slots, TW, 128), jnp.float32),
                pltpu.VMEM((slots, 128), jnp.float32),
                pltpu.VMEM((128, width), jnp.float32),
                pltpu.VMEM((4, TW, 128), jnp.float32),
                pltpu.VMEM((spikes, 128), jnp.float32),
            ],
        ),
        out_shape=[
            jax.ShapeDtypeStruct((rows, width), jnp.bfloat16),
            jax.ShapeDtypeStruct((spikes // 128, 128), jnp.float32),
            jax.ShapeDtypeStruct((owners * PACK, 128), jnp.bfloat16),
        ],
        compiler_params=pltpu.CompilerParams(
            dimension_semantics=("arbitrary",), vmem_limit_bytes=56 * 1024 * 1024
        ),
    )(
        spike_time,
        spike_template,
        slot_of,
        quot,
        rest,
        used,
        edges,
        raw,
        raw,
        raw,
        low,
        high,
        taps_row,
        whiten.T,
        temp_pairs,
        coef,
    )

    arrived = lax.all_to_all(packed.reshape(owners, PACK, 128), "tm", 0, 0)
    body_rows = CAP * TW // 2
    grads = arrived[:, :body_rows].reshape(owners * CAP, TW // 2 * 128)
    aux = arrived[:, body_rows:, :2].astype(jnp.float32).reshape(owners, 2, CAP, 2)
    weight = (aux[:, 0, :, 0] + aux[:, 1, :, 0]).reshape(slots)
    names = aux[:, 0, :, 1].reshape(slots).astype(jnp.int32)
    pick = local[:, None] == names[None, :]
    total = jnp.dot(pick.astype(jnp.bfloat16), grads, preferred_element_type=jnp.float32)
    total = total.reshape(TEMP_DEV, TW // 2, 2, NB).transpose(0, 2, 1, 3)
    total = total.reshape(TEMP_DEV, TW * NB)
    weights = jnp.sum(jnp.where(pick, weight[None, :], 0.0), axis=1)
    mine = lax.dynamic_slice_in_dim(templates, position * TEMP_DEV, TEMP_DEV, 0)
    new_templates = (mine.astype(jnp.float32) + total) / (weights[:, None] + 1.0)
    return white, amps.reshape(spikes), new_templates


def solution(mesh):
    placed = (
        P("tm", "groups"),
        P(),
        P("groups", None),
        P("groups", None),
        P("groups"),
        P("groups"),
        P(("groups", "tm")),
        P(("groups", "tm")),
        P(("groups", "tm")),
        P(("groups", "tm")),
    )
    return jax.shard_map(
        shards,
        mesh=mesh,
        in_specs=placed,
        out_specs=(P("tm", "groups"), P(("groups", "tm")), P(("groups", "tm"), None)),
        check_vma=False,
    )
```
